32 devices in a mesh: seq: 8 (over y, x, core), tp: 4 (over z).
Axes of the slice: x: 2, y: 2, z: 4, core: 2. Of those that a mesh axis runs over, the one named last changes fastest.
Arguments:
- hidden: bfloat16 [4096, 3584], P('seq', 'tp'), may hold values from -6 to 6
- modality: int32 [4096], P('seq'), may hold values from 0 to 2, as said below
- segment_bounds: int32 [6], replicated, may hold values from 0 to 4096, as said below
- block_mask: int32 [32, 32], replicated, may hold values from 0 to 1, as said below
- norm_gain: float32 [2, 2, 3584], replicated, may hold values from 0.1 to 1.9
- query_weight: bfloat16 [2, 3584, 2048], P(None, None, 'tp'), may hold values from -1 to 1
- keys_values: bfloat16 [2, 3584, 1024], P(None, None, 'tp'), may hold values from -1 to 1
- output_weight: bfloat16 [2, 2048, 3584], P(None, 'tp'), may hold values from -0.375 to 0.375
- gate_weight: bfloat16 [7168, 10240], P('seq', 'tp'), may hold values from -0.09375 to 0.09375
- up_weight: bfloat16 [7168, 10240], P('seq', 'tp'), may hold values from -0.09375 to 0.09375
- down_weight: bfloat16 [7168, 10240], P('seq', 'tp'), may hold values from -0.0625 to 0.0625
Outputs:
- layer_output: bfloat16 [4096, 3584], P('seq', 'tp')
The draws below stay inside these ranges and needn't reach their ends.
Inputs may be any that keep to these rules, and one draw needn't show every extreme that they name: `modality`: rows below 2048 carry 0 (text) or 1 (understanding image), constant over aligned runs of 32 rows; all other rows carry 2 (generation image). `segment_bounds`: strictly increasing; the first entry is 0 and the last 4096. `block_mask`: every diagonal entry is 1.
All inputs are finite; a program needn't handle non-finite values.
Results may differ from the reference program's by a relative error of at most 0.02.
The reference program's roundings to bfloat16 on the way count: a program that leaves them out, or rounds other values in their place, can miss the bound.
Values may be sent and summed in bfloat16 or wider, within the bound.
A program may use at most 192 MiB of HBM per device.

```python
import math
import jax
import jax.numpy as jnp
from jax import lax

D = 3584
FF = 10240
HEADS = 16
KVH = 4
HD = 128
BLOCK = 128
SEGS = 5
TOKENS = 4096
NB = 32
N_TP = 4


def projection_draw(key, salt, count):
    own_key = jax.random.fold_in(key, salt)
    base = jnp.clip(jax.random.normal(own_key, (2, D, count), jnp.float32), -6.0, 6.0) * D ** (-0.5)
    return base


def draw_hidden(key, part):
    own_key = jax.random.fold_in(key, 202)
    rows = jnp.clip(jax.random.normal(own_key, (TOKENS, D), jnp.float32), -6.0, 6.0)
    return rows.astype(jnp.bfloat16)


def draw_query_weight(key, part):
    return projection_draw(key, 101, HEADS * HD).astype(jnp.bfloat16)


def draw_keys_values(key, part):
    count = 2 * KVH * HD
    return projection_draw(key, 303, count).astype(jnp.bfloat16)


def draw_modality(key, part):
    half_rows = TOKENS // 2
    run_flags = jax.random.randint(key, (half_rows // 32,), 0, 2).astype(jnp.int32)
    leading = jnp.repeat(run_flags, 32)
    trailing = jnp.full((TOKENS - half_rows,), 2, jnp.int32)
    return jnp.concatenate([leading, trailing]).astype(jnp.int32)


def draw_segment_bounds(key, part):
    first_key = jax.random.fold_in(key, 11)
    rest_key = jax.random.fold_in(key, 12)
    spread = TOKENS // 16
    long_end = 3 * TOKENS // 4 + jax.random.randint(first_key, (), -spread, spread + 1).astype(jnp.int32)
    tail_length = TOKENS - long_end
    tail_count = SEGS - 1
    steps_after = jnp.arange(1, tail_count, dtype=jnp.int32)
    base_bounds = long_end + tail_length * steps_after // tail_count
    jitter = TOKENS // (16 * tail_count)
    offsets = jax.random.randint(rest_key, (tail_count - 1,), -jitter, jitter + 1).astype(jnp.int32)
    return jnp.concatenate([jnp.zeros((1,), jnp.int32), long_end.reshape(1), (base_bounds + offsets).astype(jnp.int32), jnp.full((1,), TOKENS, jnp.int32)]).astype(jnp.int32)


def draw_block_mask(key, part):
    coin_flips = jax.random.randint(key, (NB, NB), 0, 4)
    diagonal = jnp.eye(NB, dtype=jnp.int32)
    return jnp.maximum((coin_flips > 0).astype(jnp.int32), diagonal)


def levels(key, dims, cuts, least, largest):
    loudness, own = 1.0, jax.random.fold_in(key, 6)
    for axis_at, blocks in cuts:
        heights = jnp.exp(jax.random.uniform(jax.random.fold_in(own, axis_at), (blocks,), jnp.float32, least / len(cuts), largest / len(cuts)))
        loudness = loudness * jnp.repeat(heights, dims[axis_at] // blocks).reshape([-1 if axis == axis_at else 1 for axis in range(len(dims))])
    return loudness


def centred(stream_key, extent, width, limit, split=(), held_as=jnp.bfloat16):
    gain = levels(stream_key, extent, split, -0.22, 0.18) if split else 1.0
    entries = jax.random.normal(stream_key, extent, jnp.float32) * width * gain
    return jnp.minimum(jnp.maximum(entries, -limit), limit).astype(held_as)


def setup_inputs(seed: int = 0) -> dict:
    arg_keys = jax.random.split(jax.random.key(seed), 12)
    hidden = draw_hidden(jax.random.fold_in(arg_keys[11], 71), 0)
    modality = draw_modality(jax.random.fold_in(arg_keys[11], 71), 0)
    segment_bounds = draw_segment_bounds(jax.random.fold_in(arg_keys[11], 71), 0)
    block_mask = draw_block_mask(jax.random.fold_in(arg_keys[11], 71), 0)
    norm_gain = jnp.clip(1.0 + 0.18 * jax.random.normal(arg_keys[4], (2, 2, D), jnp.float32), 0.1, 1.9)
    query_weight = draw_query_weight(jax.random.fold_in(arg_keys[11], 71), 0)
    keys_values = draw_keys_values(jax.random.fold_in(arg_keys[11], 71), 0)
    output_weight = centred(arg_keys[7], (2, HEADS * HD, D), (HEADS * HD // 8) ** -0.5, 0.375, ((1, 4),))
    gate_weight = centred(arg_keys[8], (2 * D, FF), D ** -0.5, 0.09375, ((0, 8), (1, 4)))
    up_weight = centred(arg_keys[9], (2 * D, FF), D ** -0.5, 0.09375, ((0, 8), (1, 4)))
    down_weight = centred(arg_keys[10], (2 * D, FF), FF ** -0.5, 0.0625, ((0, 8), (1, 4)))
    return {"hidden": hidden, "modality": modality, "segment_bounds": segment_bounds, "block_mask": block_mask, "norm_gain": norm_gain, "query_weight": query_weight, "keys_values": keys_values, "output_weight": output_weight, "gate_weight": gate_weight, "up_weight": up_weight, "down_weight": down_weight}


theta_base = 1000000.0
epsilon = 1e-06
masked_score = -1e+30

def normalize(values, gain_row):
    widened = values.astype(jnp.float32)
    mean_square = lax.optimization_barrier(jnp.mean(widened * widened, axis=-1, keepdims=True))
    return (widened * lax.rsqrt(mean_square + epsilon) * gain_row).astype(jnp.bfloat16)

def rotary(values, offsets):
    half_dim = values.shape[-1] // 2
    frequency = theta_base ** (-2.0 * jnp.arange(half_dim, dtype=jnp.float32) / values.shape[-1])
    angles = offsets.astype(jnp.float32)[:, None] * frequency[None, :]
    cosine = jnp.cos(angles)[:, None, :]
    sine_part = jnp.sin(angles)[:, None, :]
    leading = values[..., :half_dim]
    trailing = values[..., half_dim:]
    return jnp.concatenate([leading * cosine - trailing * sine_part, trailing * cosine + leading * sine_part], axis=-1)

def segment_info(positions, segment_bounds):
    openings = segment_bounds[:-1]
    inside = positions[:, None] >= openings[None, :]
    segment_ids = lax.optimization_barrier(jnp.sum(inside.astype(jnp.int32), axis=1))
    opening = lax.optimization_barrier(jnp.max(jnp.where(inside, openings[None, :], 0), axis=1))
    return (segment_ids, positions - opening)

def sliced_sum(left_side, right_side, piece_count):
    piece_width = left_side.shape[1] // piece_count

    def accumulate(running, piece_number):
        left_piece = lax.dynamic_slice_in_dim(left_side, piece_number * piece_width, piece_width, 1)
        right_piece = lax.dynamic_slice_in_dim(right_side, piece_number * piece_width, piece_width, 0)
        rounded = lax.optimization_barrier(jnp.dot(left_piece, right_piece, preferred_element_type=jnp.float32).astype(jnp.bfloat16))
        return (running + rounded.astype(jnp.float32), None)
    initial = jnp.zeros((left_side.shape[0], right_side.shape[1]), jnp.float32)
    return lax.scan(accumulate, initial, jnp.arange(piece_count, dtype=jnp.int32))[0]

def reference(hidden, modality, segment_bounds, block_mask, norm_gain, query_weight, keys_values, output_weight, gate_weight, up_weight, down_weight):
    half_rows = TOKENS // 2
    positions = jnp.arange(TOKENS, dtype=jnp.int32)
    segment_ids, offsets = segment_info(positions, segment_bounds)
    query_parts, key_parts, value_parts = ([], [], [])
    for weight_set in range(2):
        first_row = weight_set * half_rows
        normed = normalize(hidden[first_row:first_row + half_rows], norm_gain[weight_set, 0])
        query_block = jnp.dot(normed, query_weight[weight_set], preferred_element_type=jnp.float32).reshape(half_rows, HEADS, HD)
        query_parts.append(rotary(query_block, offsets[first_row:first_row + half_rows]).astype(jnp.bfloat16))
        projected = jnp.dot(normed, keys_values[weight_set], preferred_element_type=jnp.float32).astype(jnp.bfloat16)
        raw_keys = projected[:, :KVH * HD].astype(jnp.float32).reshape(half_rows, KVH, HD)
        key_parts.append(rotary(raw_keys, offsets[first_row:first_row + half_rows]).astype(jnp.bfloat16))
        value_parts.append(projected[:, KVH * HD:].reshape(half_rows, KVH, HD))
    queries = jnp.concatenate(query_parts, 0)
    keys_all = jnp.concatenate(key_parts, 0)
    values_all = jnp.concatenate(value_parts, 0)
    group_size = HEADS // KVH
    query_step = math.gcd(TOKENS, 512)
    score_scale = HD ** (-0.5)
    key_blocks = positions // BLOCK

    def one_head(head_number):
        query_head = lax.dynamic_index_in_dim(queries, head_number, 1, keepdims=False)
        key_head = lax.dynamic_index_in_dim(keys_all, head_number // group_size, 1, keepdims=False)
        value_head = lax.dynamic_index_in_dim(values_all, head_number // group_size, 1, keepdims=False)

        def one_block(block_start):
            query_rows = lax.dynamic_slice_in_dim(query_head, block_start, query_step, 0)
            query_positions = block_start + jnp.arange(query_step, dtype=jnp.int32)
            query_segments = lax.dynamic_slice_in_dim(segment_ids, block_start, query_step, 0)
            query_modes = lax.dynamic_slice_in_dim(modality, block_start, query_step, 0)
            coarse = block_mask[(query_positions // BLOCK)[:, None], key_blocks[None, :]] == 1
            mutual = (query_modes[:, None] > 0) & (query_modes[:, None] == modality[None, :])
            allowed = coarse & (query_segments[:, None] == segment_ids[None, :]) & ((positions[None, :] <= query_positions[:, None]) | mutual)
            scores = jnp.dot(query_rows, key_head.T, preferred_element_type=jnp.float32) * score_scale
            scores = jnp.where(allowed, scores, masked_score)
            row_peak = lax.optimization_barrier(jnp.max(scores, axis=1, keepdims=True))
            exponent = jnp.where(allowed, jnp.exp(scores - row_peak), 0.0)
            mixed = jnp.dot(exponent.astype(jnp.bfloat16), value_head, preferred_element_type=jnp.float32)
            return (mixed / lax.optimization_barrier(jnp.sum(exponent, axis=1, keepdims=True))).astype(jnp.bfloat16)
        starts = jnp.arange(TOKENS // query_step, dtype=jnp.int32) * query_step
        return lax.map(one_block, starts).reshape(TOKENS, HD)
    attended = lax.map(one_head, jnp.arange(HEADS, dtype=jnp.int32))
    attended = attended.transpose(1, 0, 2).reshape(TOKENS, HEADS * HD)
    outputs = []
    for weight_set in range(2):
        first_row = weight_set * half_rows
        attention_sum = sliced_sum(attended[first_row:first_row + half_rows], output_weight[weight_set], N_TP)
        residual = (hidden[first_row:first_row + half_rows].astype(jnp.float32) + attention_sum).astype(jnp.bfloat16)
        second_normed = normalize(residual, norm_gain[weight_set, 1])
        gate_values = jnp.dot(second_normed, gate_weight[weight_set * D:(weight_set + 1) * D], preferred_element_type=jnp.float32)
        up_values = jnp.dot(second_normed, up_weight[weight_set * D:(weight_set + 1) * D], preferred_element_type=jnp.float32)
        active = (jax.nn.silu(gate_values) * up_values).astype(jnp.bfloat16)
        down_sum = sliced_sum(active, down_weight[weight_set * D:(weight_set + 1) * D].T, N_TP)
        outputs.append((residual.astype(jnp.float32) + down_sum).astype(jnp.bfloat16))
    return jnp.concatenate(outputs, 0)
```

```python
import jax
import jax.numpy as jnp
from jax import lax
from jax.experimental import pallas as pl
from jax.experimental.pallas import tpu as pltpu
from jax.sharding import PartitionSpec as P

HEADS = 16
KVH = 4
HD = 128
BLOCK = 128


theta_base = 1000000.0
epsilon = 1e-06
key_step = 512
masked_score = -1e30


def partner_2(block, axis, stride):
    count = lax.axis_size(axis)
    route = []
    for low in range(count):
        high = low | 1 << stride
        if high != low and high < count:
            route += [(low, high), (high, low)]
    return lax.ppermute(block, axis, route)


def normalize(values, gain_row):
    widened = values.astype(jnp.float32)
    mean_square = jnp.mean(widened * widened, axis=-1, keepdims=True)
    return (widened * lax.rsqrt(mean_square + epsilon) * gain_row).astype(jnp.bfloat16)


def rotary(values, offsets):
    half_dim = values.shape[-1] // 2
    frequency = theta_base ** (-2.0 * jnp.arange(half_dim, dtype=jnp.float32) / values.shape[-1])
    angles = offsets.astype(jnp.float32)[:, None] * frequency[None, :]
    cosine = jnp.cos(angles)[:, None, :]
    sine_part = jnp.sin(angles)[:, None, :]
    leading = values[..., :half_dim]
    trailing = values[..., half_dim:]
    return jnp.concatenate(
        [leading * cosine - trailing * sine_part, trailing * cosine + leading * sine_part], axis=-1
    )


def segment_info(positions, segment_bounds):
    openings = segment_bounds[:-1]
    inside = positions[:, None] >= openings[None, :]
    segment_ids = jnp.sum(inside.astype(jnp.int32), axis=1)
    opening = jnp.max(jnp.where(inside, openings[None, :], 0), axis=1)
    return (segment_ids, positions - opening)


def double_up(stacked, seq_index, level_count, partner_of):
    for bit_number in range(level_count):
        partner = partner_of(stacked, bit_number)
        upper_half = seq_index // 2**bit_number % 2 == 1
        stacked = jnp.where(
            upper_half,
            jnp.concatenate([partner, stacked], axis=1),
            jnp.concatenate([stacked, partner], axis=1),
        )
    return stacked


def general_body(
    hidden,
    modality,
    segment_bounds,
    block_mask,
    norm_gain,
    query_weight,
    keys_values,
    output_weight,
    gate_weight,
    up_weight,
    down_weight,
):
    seq_count = lax.axis_size("seq")
    seq_index = lax.axis_index("seq")
    tp_index = lax.axis_index("tp")
    row_count = hidden.shape[0]
    weight_set = (seq_index >= seq_count // 2).astype(jnp.int32)
    positions = seq_index * row_count + jnp.arange(row_count, dtype=jnp.int32)
    segment_ids, offsets = segment_info(positions, segment_bounds)
    gain_rows = lax.dynamic_index_in_dim(norm_gain, weight_set, 0, keepdims=False)
    local_query = lax.dynamic_index_in_dim(query_weight, weight_set, 0, keepdims=False)
    local_pairs = lax.dynamic_index_in_dim(keys_values, weight_set, 0, keepdims=False)
    local_output = lax.dynamic_index_in_dim(output_weight, weight_set, 0, keepdims=False)
    full_rows = lax.all_gather(hidden, "tp", axis=1, tiled=True)
    normed = normalize(full_rows, gain_rows[0])
    heads_here = local_query.shape[1] // HD
    group_size = HEADS // KVH
    shared_heads = max(1, heads_here // group_size)
    per_shared = heads_here // shared_heads
    queries = rotary(
        jnp.dot(normed, local_query, preferred_element_type=jnp.float32).reshape(
            row_count, heads_here, HD
        ),
        offsets,
    ).astype(jnp.bfloat16)
    grouped = queries.reshape(row_count, shared_heads, per_shared, HD)
    projected = jnp.dot(normed, local_pairs, preferred_element_type=jnp.float32).astype(
        jnp.bfloat16
    )
    all_pairs = lax.all_gather(projected, "tp", axis=1, tiled=True)
    first_shared = tp_index * heads_here // group_size
    raw_keys = lax.dynamic_slice_in_dim(all_pairs, first_shared * HD, shared_heads * HD, 1)
    own_values = lax.dynamic_slice_in_dim(
        all_pairs, KVH * HD + first_shared * HD, shared_heads * HD, 1
    )
    own_keys = (
        rotary(raw_keys.astype(jnp.float32).reshape(row_count, shared_heads, HD), offsets)
        .astype(jnp.bfloat16)
        .reshape(row_count, shared_heads * HD)
    )
    query_modes = modality.astype(jnp.float32)
    block_rows = row_count // BLOCK
    mask_rows = lax.dynamic_slice_in_dim(block_mask, seq_index * block_rows, block_rows, 0).astype(
        jnp.float32
    )
    block_count = block_mask.shape[1]
    score_scale = HD ** (-0.5)

    def key_block(running, key_rows, value_rows, mode_rows, key_start):
        best_score, denominator, accumulated = running
        key_count = key_rows.shape[0]
        key_positions = key_start + jnp.arange(key_count, dtype=jnp.int32)
        key_segments = segment_info(key_positions, segment_bounds)[0]
        picker = (
            key_positions[None, :] // BLOCK == jnp.arange(block_count, dtype=jnp.int32)[:, None]
        ).astype(jnp.float32)
        coarse = jnp.repeat(jnp.dot(mask_rows, picker), BLOCK, axis=0) > 0.5
        key_modes = mode_rows.astype(jnp.float32)
        mutual = (query_modes[:, None] > 0.5) & (query_modes[:, None] == key_modes[None, :])
        allowed = (
            coarse
            & (segment_ids[:, None] == key_segments[None, :])
            & ((key_positions[None, :] <= positions[:, None]) | mutual)
        )
        scores = (
            jnp.einsum(
                "rkgd,ckd->kgrc",
                grouped,
                key_rows.reshape(key_count, shared_heads, HD),
                preferred_element_type=jnp.float32,
            )
            * score_scale
        )
        scores = jnp.where(allowed[None, None], scores, masked_score)
        new_best = jnp.maximum(best_score, jnp.max(scores, axis=-1))
        exponent = jnp.where(allowed[None, None], jnp.exp(scores - new_best[..., None]), 0.0)
        fading = jnp.exp(best_score - new_best)
        denominator = denominator * fading + jnp.sum(exponent, axis=-1)
        accumulated = accumulated * fading[..., None] + jnp.einsum(
            "kgrc,ckd->kgrd",
            exponent.astype(jnp.bfloat16),
            value_rows.reshape(key_count, shared_heads, HD),
            preferred_element_type=jnp.float32,
        )
        return (new_best, denominator, accumulated)

    initial = (
        jnp.full((shared_heads, per_shared, row_count), masked_score, jnp.float32),
        jnp.zeros((shared_heads, per_shared, row_count), jnp.float32),
        jnp.zeros((shared_heads, per_shared, row_count, HD), jnp.float32),
    )
    key_rows = lax.all_gather(own_keys, "seq", axis=0, tiled=True)
    value_rows = lax.all_gather(own_values, "seq", axis=0, tiled=True)
    mode_rows = lax.all_gather(modality.astype(jnp.bfloat16), "seq", axis=0, tiled=True)
    piece_count = key_rows.shape[0]

    def one_step(step_number, inner_state):
        offset = step_number * key_step
        return key_block(
            inner_state,
            lax.dynamic_slice_in_dim(key_rows, offset, key_step, 0),
            lax.dynamic_slice_in_dim(value_rows, offset, key_step, 0),
            lax.dynamic_slice_in_dim(mode_rows, offset, key_step, 0),
            offset,
        )

    best_score, denominator, accumulated = lax.fori_loop(
        0, piece_count // key_step, one_step, initial
    )
    attended = (
        (accumulated / denominator[..., None])
        .transpose(2, 0, 1, 3)
        .reshape(row_count, heads_here * HD)
        .astype(jnp.bfloat16)
    )
    attention_terms = jnp.dot(attended, local_output, preferred_element_type=jnp.float32)
    attention_share = lax.psum_scatter(
        attention_terms.astype(jnp.bfloat16), "tp", scatter_dimension=1, tiled=True
    ).astype(jnp.float32)
    residual_share = (hidden.astype(jnp.float32) + attention_share).astype(jnp.bfloat16)
    residual_full = lax.all_gather(residual_share, "tp", axis=1, tiled=True)
    second_normed = normalize(residual_full, gain_rows[1])
    level_count = (seq_count // 2).bit_length() - 1
    paired = double_up(
        jnp.stack([gate_weight, up_weight]),
        seq_index,
        level_count,
        lambda operand, bit_number: partner_2(operand, "seq", bit_number),
    )
    down_full = double_up(
        down_weight[None],
        seq_index,
        level_count,
        lambda operand, bit_number: partner_2(operand, "seq", bit_number),
    )[0]
    gate_full, up_full = (paired[0], paired[1])
    gate_values = jnp.dot(second_normed, gate_full, preferred_element_type=jnp.float32)
    up_values = jnp.dot(second_normed, up_full, preferred_element_type=jnp.float32)
    active = (jax.nn.silu(gate_values) * up_values).astype(jnp.bfloat16)
    down_terms = lax.dot_general(
        active, down_full, (((1,), (1,)), ((), ())), preferred_element_type=jnp.float32
    )
    down_share = lax.psum_scatter(
        down_terms.astype(jnp.bfloat16), "tp", scatter_dimension=1, tiled=True
    ).astype(jnp.float32)
    return (residual_share.astype(jnp.float32) + down_share).astype(jnp.bfloat16)


def exchange(block, bit):
    count = lax.axis_size("seq")
    return lax.ppermute(block, "seq", [(low, low ^ bit) for low in range(count)])


def attend_kernel(flags, q_ref, kv_ref, bias_ref, o_ref, best, total, mixed):
    tile = pl.program_id(0)
    rows = q_ref.shape[0]
    heads = q_ref.shape[1] // HD
    stacked = jnp.concatenate([q_ref[:, h * HD : (h + 1) * HD] for h in range(heads)], axis=0)
    best[...] = jnp.full_like(best, 0.1 * masked_score)
    total[...] = jnp.zeros_like(total)
    mixed[...] = jnp.zeros_like(mixed)

    def step(chunk, carry):
        @pl.when(flags[tile, chunk] > 0)
        def _():
            span = pl.ds(pl.multiple_of(chunk * key_step, key_step), key_step)
            pair = kv_ref[span, :]
            scores = lax.dot_general(
                stacked,
                pair[:, :HD],
                (((1,), (1,)), ((), ())),
                preferred_element_type=jnp.float32,
            ) * (HD ** (-0.5))
            bias = bias_ref[:, span].astype(jnp.float32)
            scores = (scores.reshape(heads, rows, key_step) + bias[None]).reshape(
                heads * rows, key_step
            )
            old = best[...]
            peak = jnp.maximum(old, jnp.max(scores, axis=1, keepdims=True))
            fading = jnp.exp(old - peak)
            exponent = jnp.exp(scores - peak[:, :1])
            total[...] = total[...] * fading + jnp.sum(exponent, axis=1, keepdims=True)
            mixed[...] = mixed[...] * fading + jnp.dot(
                exponent.astype(jnp.bfloat16), pair[:, HD:], preferred_element_type=jnp.float32
            )
            best[...] = peak

        return carry

    lax.fori_loop(0, kv_ref.shape[0] // key_step, step, 0)
    result = (mixed[...] / total[...]).astype(jnp.bfloat16)
    for h in range(heads):
        o_ref[:, h * HD : (h + 1) * HD] = result[h * rows : (h + 1) * rows]


def attend(flags, queries, pairs, bias):
    row_count, width = queries.shape
    stacked_rows = BLOCK * (width // HD)
    return pl.pallas_call(
        attend_kernel,
        out_shape=jax.ShapeDtypeStruct((row_count, width), jnp.bfloat16),
        grid_spec=pltpu.PrefetchScalarGridSpec(
            num_scalar_prefetch=1,
            grid=(row_count // BLOCK,),
            in_specs=[
                pl.BlockSpec((BLOCK, width), lambda i, f: (i, 0)),
                pl.BlockSpec(pairs.shape, lambda i, f: (0, 0)),
                pl.BlockSpec((BLOCK, bias.shape[1]), lambda i, f: (i, 0)),
            ],
            out_specs=pl.BlockSpec((BLOCK, width), lambda i, f: (i, 0)),
            scratch_shapes=[pltpu.VMEM((stacked_rows, HD), jnp.float32)] * 3,
        ),
        compiler_params=pltpu.CompilerParams(vmem_limit_bytes=40 * 2**20),
        cost_estimate=pl.CostEstimate(
            flops=4 * row_count * width * pairs.shape[0],
            bytes_accessed=2 * pairs.size + 2 * bias.size + 4 * queries.size,
            transcendentals=row_count * width // HD * pairs.shape[0],
        ),
    )(flags, queries, pairs, bias)


def residual_kernel(places, att_ref, hidden_ref, gain_ref, *rest):
    count = (len(rest) - 4) // 1
    weights = rest[:count]
    residual_ref, normed_ref, held, sems = rest[count:]
    loads = [pltpu.make_async_copy(weights[m], held.at[m], sems.at[m]) for m in range(count)]
    for load in loads:
        load.start()
    rows, depth = att_ref.shape[1], att_ref.shape[2]
    width = hidden_ref.shape[2]
    tile = 256
    for m in range(count):
        loads[m].wait()

        def one(i, carry, m=m):
            span = pl.ds(pl.multiple_of(i * tile, tile), tile)
            terms = jnp.zeros((tile, width), jnp.float32)
            for b in range(count):
                terms += (
                    jnp.dot(att_ref[b, span, :], held[m, b], preferred_element_type=jnp.float32)
                    .astype(jnp.bfloat16)
                    .astype(jnp.float32)
                )
            row_values = hidden_ref[places[m], span, :].astype(jnp.float32)
            residual_ref[m, span, :] = (row_values + terms).astype(jnp.bfloat16)
            return carry

        lax.fori_loop(0, rows // tile, one, 0)

    def norm(i, carry):
        span = pl.ds(pl.multiple_of(i * 64, 64), 64)
        squares = jnp.zeros((64, 1), jnp.float32)
        for m in range(count):
            widened = residual_ref[m, span, :].astype(jnp.float32)
            squares += jnp.sum(widened * widened, axis=1, keepdims=True)
        scale = lax.rsqrt(squares / (count * width) + epsilon)
        for m in range(count):
            widened = residual_ref[m, span, :].astype(jnp.float32)
            normed_ref[m, span, :] = (widened * scale * gain_ref[m]).astype(jnp.bfloat16)
        return carry

    lax.fori_loop(0, rows // 64, norm, 0)


def residual_and_norm(places, attended, hidden_pieces, gains, weights):
    count = len(weights)
    vmem = pl.BlockSpec(memory_space=pltpu.VMEM)
    shape = jax.ShapeDtypeStruct(hidden_pieces.shape, jnp.bfloat16)
    return pl.pallas_call(
        residual_kernel,
        out_shape=(shape, shape),
        in_specs=[pl.BlockSpec(memory_space=pltpu.SMEM), vmem, vmem, vmem]
        + [pl.BlockSpec(memory_space=pl.ANY)] * count,
        out_specs=(vmem, vmem),
        scratch_shapes=[
            pltpu.VMEM((count,) + weights[0].shape, jnp.bfloat16),
            pltpu.SemaphoreType.DMA((count,)),
        ],
        compiler_params=pltpu.CompilerParams(vmem_limit_bytes=48 * 2**20),
        cost_estimate=pl.CostEstimate(
            flops=2 * attended.size * hidden_pieces.shape[2] * count,
            bytes_accessed=2 * count * weights[0].size + 6 * hidden_pieces.size,
            transcendentals=0,
        ),
    )(places, attended, hidden_pieces, gains, *weights)


def gate_up_kernel(x_ref, *rest):
    out_ref = rest[-1]
    count = x_ref.shape[0]
    gate = jnp.zeros(out_ref.shape, jnp.float32)
    up = jnp.zeros(out_ref.shape, jnp.float32)
    for m in range(count):
        gate += jnp.dot(x_ref[m], rest[m][...], preferred_element_type=jnp.float32)
    for m in range(count):
        up += jnp.dot(x_ref[m], rest[count + m][...], preferred_element_type=jnp.float32)
    out_ref[...] = (gate / (1.0 + jnp.exp(-gate)) * up).astype(jnp.bfloat16)


def gate_up(x, gates, ups):
    count, rows, depth = x.shape
    hidden_units = gates[0].shape[1]
    tile = 256
    return pl.pallas_call(
        gate_up_kernel,
        out_shape=jax.ShapeDtypeStruct((rows, hidden_units), jnp.bfloat16),
        grid=(hidden_units // tile,),
        in_specs=[pl.BlockSpec(x.shape, lambda i: (0, 0, 0))]
        + [pl.BlockSpec((depth, tile), lambda i: (0, i))] * (2 * count),
        out_specs=pl.BlockSpec((rows, tile), lambda i: (0, i)),
        compiler_params=pltpu.CompilerParams(vmem_limit_bytes=48 * 2**20),
        cost_estimate=pl.CostEstimate(
            flops=4 * x.size * hidden_units,
            bytes_accessed=4 * count * gates[0].size + 2 * x.size,
            transcendentals=rows * hidden_units,
        ),
    )(x, *gates, *ups)


def down_kernel(places, active_ref, *rest):
    count = len(rest) - 3
    weights = rest[:count]
    out_ref, held, sems = rest[count:]
    loads = [pltpu.make_async_copy(weights[m], held.at[m], sems.at[m]) for m in range(count)]
    for load in loads:
        load.start()
    tile = 256
    for m in range(count):
        loads[m].wait()

        def one(i, carry, m=m):
            span = pl.ds(pl.multiple_of(i * tile, tile), tile)
            out_ref[places[m], span, :] = lax.dot_general(
                active_ref[span, :],
                held[m],
                (((1,), (1,)), ((), ())),
                preferred_element_type=jnp.float32,
            ).astype(jnp.bfloat16)
            return carry

        lax.fori_loop(0, active_ref.shape[0] // tile, one, 0)


def down_terms_of(places, active, weights):
    count = len(weights)
    rows = active.shape[0]
    width = weights[0].shape[0]
    vmem = pl.BlockSpec(memory_space=pltpu.VMEM)
    return pl.pallas_call(
        down_kernel,
        out_shape=jax.ShapeDtypeStruct((count, rows, width), jnp.bfloat16),
        in_specs=[pl.BlockSpec(memory_space=pltpu.SMEM), vmem]
        + [pl.BlockSpec(memory_space=pl.ANY)] * count,
        out_specs=vmem,
        scratch_shapes=[
            pltpu.VMEM((count,) + weights[0].shape, jnp.bfloat16),
            pltpu.SemaphoreType.DMA((count,)),
        ],
        compiler_params=pltpu.CompilerParams(vmem_limit_bytes=48 * 2**20),
        cost_estimate=pl.CostEstimate(
            flops=2 * active.size * width * count,
            bytes_accessed=2 * count * weights[0].size + 2 * active.size,
            transcendentals=0,
        ),
    )(places, active, *weights)


def square_body(
    hidden,
    modality,
    segment_bounds,
    block_mask,
    norm_gain,
    query_weight,
    keys_values,
    output_weight,
    gate_weight,
    up_weight,
    down_weight,
):
    seq_count = lax.axis_size("seq")
    seq_index = lax.axis_index("seq")
    tp_index = lax.axis_index("tp")
    group = seq_count // 2
    row_count, width = hidden.shape
    weight_set = (seq_index >= group).astype(jnp.int32)
    member = seq_index % group
    places = member ^ jnp.arange(group, dtype=jnp.int32)
    positions = seq_index * row_count + jnp.arange(row_count, dtype=jnp.int32)
    segment_ids, offsets = segment_info(positions, segment_bounds)
    gain_rows = lax.dynamic_index_in_dim(norm_gain, weight_set, 0, keepdims=False)
    local_query = lax.dynamic_index_in_dim(query_weight, weight_set, 0, keepdims=False)
    local_pairs = lax.dynamic_index_in_dim(keys_values, weight_set, 0, keepdims=False)

    hidden_pieces = lax.all_gather(hidden, "tp", axis=0, tiled=False)
    gate_far = exchange(gate_weight, 2)
    up_far = exchange(up_weight, 2)
    gate_near = exchange(gate_weight, 1)
    up_near = exchange(up_weight, 1)
    modes = lax.all_gather(modality, "seq", axis=0, tiled=True)

    key_count = modes.shape[0]
    key_positions = jnp.arange(key_count, dtype=jnp.int32)
    key_segments = segment_info(key_positions, segment_bounds)[0]
    block_rows = row_count // BLOCK
    mask_rows = lax.dynamic_slice_in_dim(block_mask, seq_index * block_rows, block_rows, 0)
    coarse = jnp.broadcast_to(
        (mask_rows == 1)[:, None, :, None], (block_rows, BLOCK, key_count // BLOCK, BLOCK)
    ).reshape(row_count, key_count)
    mutual = (modality[:, None] > 0) & (modality[:, None] == modes[None, :])
    allowed = (
        coarse
        & (segment_ids[:, None] == key_segments[None, :])
        & ((key_positions[None, :] <= positions[:, None]) | mutual)
    )
    bias = jnp.where(allowed, 0.0, masked_score).astype(jnp.bfloat16)
    flags = jnp.any(
        allowed.reshape(block_rows, BLOCK, key_count // key_step, key_step), axis=(1, 3)
    ).astype(jnp.int32)

    full_rows = jnp.concatenate([hidden_pieces[c] for c in range(group)], axis=1)
    normed = normalize(full_rows, gain_rows[0])
    projected = jnp.dot(normed, local_pairs, preferred_element_type=jnp.float32).astype(
        jnp.bfloat16
    )
    edge = (tp_index == 0) | (tp_index == 3)
    left_part, right_part = projected[:, :HD], projected[:, HD:]
    first = lax.ppermute(
        jnp.where(edge, right_part, left_part), "tp", [(0, 1), (1, 2), (2, 0), (3, 3)]
    )
    second = lax.ppermute(
        jnp.where(edge, left_part, right_part), "tp", [(0, 0), (1, 3), (2, 1), (3, 2)]
    )
    raw_keys = jnp.where(edge, second, first)
    own_values = jnp.where(edge, first, second)
    own_keys = rotary(raw_keys.astype(jnp.float32)[:, None, :], offsets)[:, 0, :].astype(
        jnp.bfloat16
    )
    pairs = lax.all_gather(
        jnp.concatenate([own_keys, own_values], axis=1), "seq", axis=0, tiled=True
    )
    queries = (
        rotary(
            jnp.dot(normed, local_query, preferred_element_type=jnp.float32).reshape(
                row_count, -1, HD
            ),
            offsets,
        )
        .astype(jnp.bfloat16)
        .reshape(row_count, -1)
    )

    output_slice = lax.dynamic_slice(
        output_weight,
        (weight_set, 0, member * width),
        (1, output_weight.shape[1], width),
    )[0]
    output_slice, projected_tied = lax.optimization_barrier((output_slice, projected))
    output_own = lax.all_gather(output_slice, "tp", axis=0, tiled=False)
    output_far = exchange(output_own, 2)
    output_near = exchange(output_own, 1)
    output_diagonal = exchange(output_far, 1)
    down_tied, output_own = lax.optimization_barrier((down_weight, output_own))
    down_far = exchange(down_tied, 2)
    down_near = exchange(down_tied, 1)

    gate_far, up_far, pairs = lax.optimization_barrier((gate_far, up_far, pairs))
    gate_diagonal = exchange(gate_far, 1)
    up_diagonal = exchange(up_far, 1)

    attended = attend(flags, queries, pairs, bias)
    attended_all = lax.all_gather(attended, "tp", axis=0, tiled=False)
    gains = gain_rows[1].reshape(group, 1, width)[places]
    residual_pieces, normed_pieces = residual_and_norm(
        places,
        attended_all,
        hidden_pieces,
        gains,
        (output_own, output_near, output_far, output_diagonal),
    )
    down_far, normed_pieces = lax.optimization_barrier((down_far, normed_pieces))
    down_diagonal = exchange(down_far, 1)
    active = gate_up(
        normed_pieces,
        (gate_weight, gate_near, gate_far, gate_diagonal),
        (up_weight, up_near, up_far, up_diagonal),
    )
    terms = down_terms_of(places, active, (down_weight, down_near, down_far, down_diagonal))
    down_share = lax.psum_scatter(terms, "tp", scatter_dimension=0, tiled=False)
    residual_share = lax.dynamic_index_in_dim(
        residual_pieces, member ^ tp_index, 0, keepdims=False
    )
    return (residual_share.astype(jnp.float32) + down_share.astype(jnp.float32)).astype(
        jnp.bfloat16
    )


def solution(mesh):
    placed = (
        P("seq", "tp"),
        P("seq"),
        P(),
        P(),
        P(),
        P(None, None, "tp"),
        P(None, None, "tp"),
        P(None, "tp", None),
        P("seq", "tp"),
        P("seq", "tp"),
        P("seq", "tp"),
    )
    square = mesh.shape["seq"] == 2 * KVH and mesh.shape["tp"] == KVH
    return jax.shard_map(
        square_body if square else general_body, mesh=mesh, in_specs=placed, out_specs=P("seq", "tp"), check_vma=False
    )
```

```python
import functools

import jax
import jax.numpy as jnp
from jax import lax
from jax.experimental import pallas as pl
from jax.experimental.pallas import tpu as pltpu
from jax.sharding import PartitionSpec as P

HEADS = 16
KVH = 4
HD = 128
BLOCK = 128


theta_base = 1000000.0
epsilon = 1e-06
key_step = 512
masked_score = -1e30


def partner_2(block, axis, stride):
    count = lax.axis_size(axis)
    route = []
    for low in range(count):
        high = low | 1 << stride
        if high != low and high < count:
            route += [(low, high), (high, low)]
    return lax.ppermute(block, axis, route)


def normalize(values, gain_row):
    widened = values.astype(jnp.float32)
    mean_square = jnp.mean(widened * widened, axis=-1, keepdims=True)
    return (widened * lax.rsqrt(mean_square + epsilon) * gain_row).astype(jnp.bfloat16)


def rotary(values, offsets):
    half_dim = values.shape[-1] // 2
    frequency = theta_base ** (-2.0 * jnp.arange(half_dim, dtype=jnp.float32) / values.shape[-1])
    angles = offsets.astype(jnp.float32)[:, None] * frequency[None, :]
    cosine = jnp.cos(angles)[:, None, :]
    sine_part = jnp.sin(angles)[:, None, :]
    leading = values[..., :half_dim]
    trailing = values[..., half_dim:]
    return jnp.concatenate(
        [leading * cosine - trailing * sine_part, trailing * cosine + leading * sine_part], axis=-1
    )


def segment_info(positions, segment_bounds):
    openings = segment_bounds[:-1]
    inside = positions[:, None] >= openings[None, :]
    segment_ids = jnp.sum(inside.astype(jnp.int32), axis=1)
    opening = jnp.max(jnp.where(inside, openings[None, :], 0), axis=1)
    return (segment_ids, positions - opening)


def double_up(stacked, seq_index, level_count, partner_of):
    for bit_number in range(level_count):
        partner = partner_of(stacked, bit_number)
        upper_half = seq_index // 2**bit_number % 2 == 1
        stacked = jnp.where(
            upper_half,
            jnp.concatenate([partner, stacked], axis=1),
            jnp.concatenate([stacked, partner], axis=1),
        )
    return stacked


def general_body(
    hidden,
    modality,
    segment_bounds,
    block_mask,
    norm_gain,
    query_weight,
    keys_values,
    output_weight,
    gate_weight,
    up_weight,
    down_weight,
):
    seq_count = lax.axis_size("seq")
    seq_index = lax.axis_index("seq")
    tp_index = lax.axis_index("tp")
    row_count = hidden.shape[0]
    weight_set = (seq_index >= seq_count // 2).astype(jnp.int32)
    positions = seq_index * row_count + jnp.arange(row_count, dtype=jnp.int32)
    segment_ids, offsets = segment_info(positions, segment_bounds)
    gain_rows = lax.dynamic_index_in_dim(norm_gain, weight_set, 0, keepdims=False)
    local_query = lax.dynamic_index_in_dim(query_weight, weight_set, 0, keepdims=False)
    local_pairs = lax.dynamic_index_in_dim(keys_values, weight_set, 0, keepdims=False)
    local_output = lax.dynamic_index_in_dim(output_weight, weight_set, 0, keepdims=False)
    full_rows = lax.all_gather(hidden, "tp", axis=1, tiled=True)
    normed = normalize(full_rows, gain_rows[0])
    heads_here = local_query.shape[1] // HD
    group_size = HEADS // KVH
    shared_heads = max(1, heads_here // group_size)
    per_shared = heads_here // shared_heads
    queries = rotary(
        jnp.dot(normed, local_query, preferred_element_type=jnp.float32).reshape(
            row_count, heads_here, HD
        ),
        offsets,
    ).astype(jnp.bfloat16)
    grouped = queries.reshape(row_count, shared_heads, per_shared, HD)
    projected = jnp.dot(normed, local_pairs, preferred_element_type=jnp.float32).astype(
        jnp.bfloat16
    )
    all_pairs = lax.all_gather(projected, "tp", axis=1, tiled=True)
    first_shared = tp_index * heads_here // group_size
    raw_keys = lax.dynamic_slice_in_dim(all_pairs, first_shared * HD, shared_heads * HD, 1)
    own_values = lax.dynamic_slice_in_dim(
        all_pairs, KVH * HD + first_shared * HD, shared_heads * HD, 1
    )
    own_keys = (
        rotary(raw_keys.astype(jnp.float32).reshape(row_count, shared_heads, HD), offsets)
        .astype(jnp.bfloat16)
        .reshape(row_count, shared_heads * HD)
    )
    query_modes = modality.astype(jnp.float32)
    block_rows = row_count // BLOCK
    mask_rows = lax.dynamic_slice_in_dim(block_mask, seq_index * block_rows, block_rows, 0).astype(
        jnp.float32
    )
    block_count = block_mask.shape[1]
    score_scale = HD ** (-0.5)

    def key_block(running, key_rows, value_rows, mode_rows, key_start):
        best_score, denominator, accumulated = running
        key_count = key_rows.shape[0]
        key_positions = key_start + jnp.arange(key_count, dtype=jnp.int32)
        key_segments = segment_info(key_positions, segment_bounds)[0]
        picker = (
            key_positions[None, :] // BLOCK == jnp.arange(block_count, dtype=jnp.int32)[:, None]
        ).astype(jnp.float32)
        coarse = jnp.repeat(jnp.dot(mask_rows, picker), BLOCK, axis=0) > 0.5
        key_modes = mode_rows.astype(jnp.float32)
        mutual = (query_modes[:, None] > 0.5) & (query_modes[:, None] == key_modes[None, :])
        allowed = (
            coarse
            & (segment_ids[:, None] == key_segments[None, :])
            & ((key_positions[None, :] <= positions[:, None]) | mutual)
        )
        scores = (
            jnp.einsum(
                "rkgd,ckd->kgrc",
                grouped,
                key_rows.reshape(key_count, shared_heads, HD),
                preferred_element_type=jnp.float32,
            )
            * score_scale
        )
        scores = jnp.where(allowed[None, None], scores, masked_score)
        new_best = jnp.maximum(best_score, jnp.max(scores, axis=-1))
        exponent = jnp.where(allowed[None, None], jnp.exp(scores - new_best[..., None]), 0.0)
        fading = jnp.exp(best_score - new_best)
        denominator = denominator * fading + jnp.sum(exponent, axis=-1)
        accumulated = accumulated * fading[..., None] + jnp.einsum(
            "kgrc,ckd->kgrd",
            exponent.astype(jnp.bfloat16),
            value_rows.reshape(key_count, shared_heads, HD),
            preferred_element_type=jnp.float32,
        )
        return (new_best, denominator, accumulated)

    initial = (
        jnp.full((shared_heads, per_shared, row_count), masked_score, jnp.float32),
        jnp.zeros((shared_heads, per_shared, row_count), jnp.float32),
        jnp.zeros((shared_heads, per_shared, row_count, HD), jnp.float32),
    )
    key_rows = lax.all_gather(own_keys, "seq", axis=0, tiled=True)
    value_rows = lax.all_gather(own_values, "seq", axis=0, tiled=True)
    mode_rows = lax.all_gather(modality.astype(jnp.bfloat16), "seq", axis=0, tiled=True)
    piece_count = key_rows.shape[0]

    def one_step(step_number, inner_state):
        offset = step_number * key_step
        return key_block(
            inner_state,
            lax.dynamic_slice_in_dim(key_rows, offset, key_step, 0),
            lax.dynamic_slice_in_dim(value_rows, offset, key_step, 0),
            lax.dynamic_slice_in_dim(mode_rows, offset, key_step, 0),
            offset,
        )

    best_score, denominator, accumulated = lax.fori_loop(
        0, piece_count // key_step, one_step, initial
    )
    attended = (
        (accumulated / denominator[..., None])
        .transpose(2, 0, 1, 3)
        .reshape(row_count, heads_here * HD)
        .astype(jnp.bfloat16)
    )
    attention_terms = jnp.dot(attended, local_output, preferred_element_type=jnp.float32)
    attention_share = lax.psum_scatter(
        attention_terms.astype(jnp.bfloat16), "tp", scatter_dimension=1, tiled=True
    ).astype(jnp.float32)
    residual_share = (hidden.astype(jnp.float32) + attention_share).astype(jnp.bfloat16)
    residual_full = lax.all_gather(residual_share, "tp", axis=1, tiled=True)
    second_normed = normalize(residual_full, gain_rows[1])
    level_count = (seq_count // 2).bit_length() - 1
    paired = double_up(
        jnp.stack([gate_weight, up_weight]),
        seq_index,
        level_count,
        lambda operand, bit_number: partner_2(operand, "seq", bit_number),
    )
    down_full = double_up(
        down_weight[None],
        seq_index,
        level_count,
        lambda operand, bit_number: partner_2(operand, "seq", bit_number),
    )[0]
    gate_full, up_full = (paired[0], paired[1])
    gate_values = jnp.dot(second_normed, gate_full, preferred_element_type=jnp.float32)
    up_values = jnp.dot(second_normed, up_full, preferred_element_type=jnp.float32)
    active = (jax.nn.silu(gate_values) * up_values).astype(jnp.bfloat16)
    down_terms = lax.dot_general(
        active, down_full, (((1,), (1,)), ((), ())), preferred_element_type=jnp.float32
    )
    down_share = lax.psum_scatter(
        down_terms.astype(jnp.bfloat16), "tp", scatter_dimension=1, tiled=True
    ).astype(jnp.float32)
    return (residual_share.astype(jnp.float32) + down_share).astype(jnp.bfloat16)


def exchange(block, bit):
    count = lax.axis_size("seq")
    return lax.ppermute(block, "seq", [(low, low ^ bit) for low in range(count)])


def attend_kernel(flags, q_ref, kv_ref, bias_ref, o_ref, best, total, mixed):
    tile = pl.program_id(0)
    rows = q_ref.shape[0]
    heads = q_ref.shape[1] // HD
    stacked = jnp.concatenate([q_ref[:, h * HD : (h + 1) * HD] for h in range(heads)], axis=0)
    best[...] = jnp.full_like(best, 0.1 * masked_score)
    total[...] = jnp.zeros_like(total)
    mixed[...] = jnp.zeros_like(mixed)

    def step(chunk, carry):
        @pl.when(flags[tile, chunk] > 0)
        def _():
            span = pl.ds(pl.multiple_of(chunk * key_step, key_step), key_step)
            pair = kv_ref[span, :]
            scores = lax.dot_general(
                stacked,
                pair[:, :HD],
                (((1,), (1,)), ((), ())),
                preferred_element_type=jnp.float32,
            ) * (HD ** (-0.5))
            bias = bias_ref[:, span].astype(jnp.float32)
            scores = (scores.reshape(heads, rows, key_step) + bias[None]).reshape(
                heads * rows, key_step
            )
            old = best[...]
            peak = jnp.maximum(old, jnp.max(scores, axis=1, keepdims=True))
            fading = jnp.exp(old - peak)
            exponent = jnp.exp(scores - peak[:, :1])
            total[...] = total[...] * fading + jnp.sum(exponent, axis=1, keepdims=True)
            mixed[...] = mixed[...] * fading + jnp.dot(
                exponent.astype(jnp.bfloat16), pair[:, HD:], preferred_element_type=jnp.float32
            )
            best[...] = peak

        return carry

    lax.fori_loop(0, kv_ref.shape[0] // key_step, step, 0)
    result = (mixed[...] / total[...]).astype(jnp.bfloat16)
    for h in range(heads):
        o_ref[:, h * HD : (h + 1) * HD] = result[h * rows : (h + 1) * rows]


def attend(flags, queries, pairs, bias):
    row_count, width = queries.shape
    stacked_rows = BLOCK * (width // HD)
    return pl.pallas_call(
        attend_kernel,
        out_shape=jax.ShapeDtypeStruct((row_count, width), jnp.bfloat16),
        grid_spec=pltpu.PrefetchScalarGridSpec(
            num_scalar_prefetch=1,
            grid=(row_count // BLOCK,),
            in_specs=[
                pl.BlockSpec((BLOCK, width), lambda i, f: (i, 0)),
                pl.BlockSpec(pairs.shape, lambda i, f: (0, 0)),
                pl.BlockSpec((BLOCK, bias.shape[1]), lambda i, f: (i, 0)),
            ],
            out_specs=pl.BlockSpec((BLOCK, width), lambda i, f: (i, 0)),
            scratch_shapes=[pltpu.VMEM((stacked_rows, HD), jnp.float32)] * 3,
        ),
        compiler_params=pltpu.CompilerParams(vmem_limit_bytes=40 * 2**20),
        cost_estimate=pl.CostEstimate(
            flops=4 * row_count * width * pairs.shape[0],
            bytes_accessed=2 * pairs.size + 2 * bias.size + 4 * queries.size,
            transcendentals=row_count * width // HD * pairs.shape[0],
        ),
    )(flags, queries, pairs, bias)


def output_kernel(chosen, att_ref, weight_ref, out_ref):
    out_ref[0] = jnp.dot(
        att_ref[...], weight_ref[0], preferred_element_type=jnp.float32
    ).astype(jnp.bfloat16)


def output_terms(chosen, attended, output_weight, width):
    rows, depth = attended.shape
    count = output_weight.shape[2] // width
    return pl.pallas_call(
        output_kernel,
        out_shape=jax.ShapeDtypeStruct((count, rows, width), jnp.bfloat16),
        grid_spec=pltpu.PrefetchScalarGridSpec(
            num_scalar_prefetch=1,
            grid=(count,),
            in_specs=[
                pl.BlockSpec((rows, depth), lambda c, f: (0, 0)),
                pl.BlockSpec((1, depth, width), lambda c, f: (f[0], 0, c)),
            ],
            out_specs=pl.BlockSpec((1, rows, width), lambda c, f: (c, 0, 0)),
        ),
        compiler_params=pltpu.CompilerParams(vmem_limit_bytes=32 * 2**20),
        cost_estimate=pl.CostEstimate(
            flops=2 * attended.size * width * count,
            bytes_accessed=2 * depth * width * count + 2 * rows * width * count,
            transcendentals=0,
        ),
    )(chosen, attended, output_weight)


def gate_up_kernel(counts, places, x_ref, *rest):
    out_ref = rest[-1]
    at = 0
    totals = []
    for layout in counts:
        total = jnp.zeros(out_ref.shape, jnp.float32)
        for m, parts in enumerate(layout):
            first = 0
            for depth in parts:
                total += jnp.dot(
                    x_ref[places[m], :, first : first + depth],
                    rest[at][...],
                    preferred_element_type=jnp.float32,
                )
                first += depth
                at += 1
        totals.append(total)
    gate, up = totals
    out_ref[...] = (gate / (1.0 + jnp.exp(-gate)) * up).astype(jnp.bfloat16)


def gate_up(places, x, gates, ups):
    count, rows, depth = x.shape
    arrays = [part for piece in gates + ups for part in piece]
    counts = [[[part.shape[0] for part in piece] for piece in pieces] for pieces in (gates, ups)]
    hidden_units = arrays[0].shape[1]
    tile = 256
    return pl.pallas_call(
        functools.partial(gate_up_kernel, counts),
        out_shape=jax.ShapeDtypeStruct((rows, hidden_units), jnp.bfloat16),
        grid_spec=pltpu.PrefetchScalarGridSpec(
            num_scalar_prefetch=1,
            grid=(hidden_units // tile,),
            in_specs=[pl.BlockSpec(x.shape, lambda i, f: (0, 0, 0))]
            + [pl.BlockSpec((part.shape[0], tile), lambda i, f: (0, i)) for part in arrays],
            out_specs=pl.BlockSpec((rows, tile), lambda i, f: (0, i)),
        ),
        compiler_params=pltpu.CompilerParams(vmem_limit_bytes=48 * 2**20),
        cost_estimate=pl.CostEstimate(
            flops=4 * x.size * hidden_units,
            bytes_accessed=4 * count * depth * hidden_units + 2 * x.size,
            transcendentals=rows * hidden_units,
        ),
    )(places, x, *arrays)


def down_kernel(counts, places, active_ref, *rest):
    total = sum(len(parts) for parts in counts)
    weights = rest[:total]
    out_ref, held, sems = rest[total:]
    loads = []
    at = 0
    for m, parts in enumerate(counts):
        first = 0
        for depth in parts:
            loads.append(
                pltpu.make_async_copy(
                    weights[at], held.at[m, first : first + depth], sems.at[at]
                )
            )
            first += depth
            at += 1
    for load in loads:
        load.start()
    tile = 256
    at = 0
    for m, parts in enumerate(counts):
        for _ in parts:
            loads[at].wait()
            at += 1

        def one(i, carry, m=m):
            span = pl.ds(pl.multiple_of(i * tile, tile), tile)
            out_ref[places[m], span, :] = lax.dot_general(
                active_ref[span, :],
                held[m],
                (((1,), (1,)), ((), ())),
                preferred_element_type=jnp.float32,
            ).astype(jnp.bfloat16)
            return carry

        lax.fori_loop(0, active_ref.shape[0] // tile, one, 0)


def down_terms_of(places, active, pieces):
    count = len(pieces)
    rows, hidden_units = active.shape
    arrays = [part for piece in pieces for part in piece]
    counts = [[part.shape[0] for part in piece] for piece in pieces]
    width = sum(counts[0])
    vmem = pl.BlockSpec(memory_space=pltpu.VMEM)
    return pl.pallas_call(
        functools.partial(down_kernel, counts),
        out_shape=jax.ShapeDtypeStruct((count, rows, width), jnp.bfloat16),
        in_specs=[pl.BlockSpec(memory_space=pltpu.SMEM), vmem]
        + [pl.BlockSpec(memory_space=pl.ANY)] * len(arrays),
        out_specs=vmem,
        scratch_shapes=[
            pltpu.VMEM((count, width, hidden_units), jnp.bfloat16),
            pltpu.SemaphoreType.DMA((len(arrays),)),
        ],
        compiler_params=pltpu.CompilerParams(vmem_limit_bytes=48 * 2**20),
        cost_estimate=pl.CostEstimate(
            flops=2 * active.size * width * count,
            bytes_accessed=2 * count * width * hidden_units + 2 * active.size,
            transcendentals=0,
        ),
    )(places, active, *arrays)


def square_body(
    hidden,
    modality,
    segment_bounds,
    block_mask,
    norm_gain,
    query_weight,
    keys_values,
    output_weight,
    gate_weight,
    up_weight,
    down_weight,
):
    seq_count = lax.axis_size("seq")
    seq_index = lax.axis_index("seq")
    tp_index = lax.axis_index("tp")
    group = seq_count // 2
    row_count, width = hidden.shape
    weight_set = (seq_index >= group).astype(jnp.int32)
    member = seq_index % group
    places = member ^ jnp.arange(group, dtype=jnp.int32)
    positions = seq_index * row_count + jnp.arange(row_count, dtype=jnp.int32)
    segment_ids, offsets = segment_info(positions, segment_bounds)
    gain_rows = lax.dynamic_index_in_dim(norm_gain, weight_set, 0, keepdims=False)
    local_query = lax.dynamic_index_in_dim(query_weight, weight_set, 0, keepdims=False)
    local_pairs = lax.dynamic_index_in_dim(keys_values, weight_set, 0, keepdims=False)

    modes = lax.all_gather(modality, "seq", axis=0, tiled=True)
    gate_tied, modes = lax.optimization_barrier((gate_weight, modes))
    hidden_pieces = lax.all_gather(hidden, "tp", axis=0, tiled=False)
    depth = gate_weight.shape[0]
    long_cut = depth * 5 // 7 // 128 * 128
    short_cut = depth - long_cut
    gate_far_a = exchange(gate_tied[:long_cut], 2)
    gate_far_b = exchange(gate_tied[long_cut:], 2)
    hidden_pieces, gate_far_a = lax.optimization_barrier((hidden_pieces, gate_far_a))
    gate_near = exchange(gate_weight, 1)
    up_near = exchange(up_weight, 1)

    key_count = modes.shape[0]
    key_positions = jnp.arange(key_count, dtype=jnp.int32)
    key_segments = segment_info(key_positions, segment_bounds)[0]
    block_rows = row_count // BLOCK
    mask_rows = lax.dynamic_slice_in_dim(block_mask, seq_index * block_rows, block_rows, 0)
    coarse = jnp.broadcast_to(
        (mask_rows == 1)[:, None, :, None], (block_rows, BLOCK, key_count // BLOCK, BLOCK)
    ).reshape(row_count, key_count)
    mutual = (modality[:, None] > 0) & (modality[:, None] == modes[None, :])
    allowed = (
        coarse
        & (segment_ids[:, None] == key_segments[None, :])
        & ((key_positions[None, :] <= positions[:, None]) | mutual)
    )
    bias = jnp.where(allowed, 0.0, masked_score).astype(jnp.bfloat16)
    flags = jnp.any(
        allowed.reshape(block_rows, BLOCK, key_count // key_step, key_step), axis=(1, 3)
    ).astype(jnp.int32)

    full_rows = jnp.concatenate([hidden_pieces[c] for c in range(group)], axis=1)
    normed = normalize(full_rows, gain_rows[0])
    projected = jnp.dot(normed, local_pairs, preferred_element_type=jnp.float32).astype(
        jnp.bfloat16
    )
    edge = (tp_index == 0) | (tp_index == 3)
    left_part, right_part = projected[:, :HD], projected[:, HD:]
    first = lax.ppermute(
        jnp.where(edge, right_part, left_part), "tp", [(0, 1), (1, 2), (2, 0), (3, 3)]
    )
    second = lax.ppermute(
        jnp.where(edge, left_part, right_part), "tp", [(0, 0), (1, 3), (2, 1), (3, 2)]
    )
    raw_keys = jnp.where(edge, second, first)
    own_values = jnp.where(edge, first, second)
    own_keys = rotary(raw_keys.astype(jnp.float32)[:, None, :], offsets)[:, 0, :].astype(
        jnp.bfloat16
    )
    own_pairs = jnp.concatenate([own_keys, own_values], axis=1)
    own_pairs, gate_far_b = lax.optimization_barrier((own_pairs, gate_far_b))
    pairs = lax.all_gather(own_pairs, "seq", axis=0, tiled=True)
    pairs, up_tied, down_tied, gate_far_a, gate_far_b = lax.optimization_barrier(
        (pairs, up_weight, down_weight, gate_far_a, gate_far_b)
    )
    up_far_a = exchange(up_tied[:short_cut], 2)
    up_far_b = exchange(up_tied[short_cut:], 2)
    gate_diagonal_a = exchange(gate_far_a, 1)
    gate_diagonal_b = exchange(gate_far_b, 1)
    queries = (
        rotary(
            jnp.dot(normed, local_query, preferred_element_type=jnp.float32).reshape(
                row_count, -1, HD
            ),
            offsets,
        )
        .astype(jnp.bfloat16)
        .reshape(row_count, -1)
    )

    attended = attend(flags, queries, pairs, bias)
    attended, up_far_a, down_tied = lax.optimization_barrier((attended, up_far_a, down_tied))
    up_diagonal_a = exchange(up_far_a, 1)
    down_near = exchange(down_tied, 1)
    half = depth // 2
    down_far_a = exchange(down_tied[:half], 2)
    down_far_b = exchange(down_tied[half:], 2)
    attention_terms = output_terms(weight_set[None], attended, output_weight, width)
    attention_share = lax.psum_scatter(attention_terms, "tp", scatter_dimension=0, tiled=False)
    attention_share, up_far_b = lax.optimization_barrier((attention_share, up_far_b))
    up_diagonal_b = exchange(up_far_b, 1)
    residual_share = (hidden.astype(jnp.float32) + attention_share.astype(jnp.float32)).astype(
        jnp.bfloat16
    )
    residual_pieces = lax.all_gather(residual_share, "tp", axis=0, tiled=False)
    residual_pieces, down_far_a = lax.optimization_barrier((residual_pieces, down_far_a))
    down_diagonal_a = exchange(down_far_a, 1)
    widened = residual_pieces.astype(jnp.float32)
    mean_square = jnp.mean(widened * widened, axis=(0, 2), keepdims=True)
    gains = gain_rows[1].reshape(group, 1, width)
    second_normed = (widened * lax.rsqrt(mean_square + epsilon) * gains).astype(jnp.bfloat16)
    active = gate_up(
        places,
        second_normed,
        [[gate_weight], [gate_near], [gate_far_a, gate_far_b], [gate_diagonal_a, gate_diagonal_b]],
        [[up_weight], [up_near], [up_far_a, up_far_b], [up_diagonal_a, up_diagonal_b]],
    )
    down_diagonal_b = exchange(down_far_b, 1)
    terms = down_terms_of(
        places,
        active,
        [[down_weight], [down_near], [down_far_a, down_far_b], [down_diagonal_a, down_diagonal_b]],
    )
    down_share = lax.psum_scatter(terms, "tp", scatter_dimension=0, tiled=False)
    return (residual_share.astype(jnp.float32) + down_share.astype(jnp.float32)).astype(
        jnp.bfloat16
    )


def solution(mesh):
    placed = (
        P("seq", "tp"),
        P("seq"),
        P(),
        P(),
        P(),
        P(None, None, "tp"),
        P(None, None, "tp"),
        P(None, "tp", None),
        P("seq", "tp"),
        P("seq", "tp"),
        P("seq", "tp"),
    )
    square = mesh.shape["seq"] == 2 * KVH and mesh.shape["tp"] == KVH
    return jax.shard_map(
        square_body if square else general_body, mesh=mesh, in_specs=placed, out_specs=P("seq", "tp"), check_vma=False
    )
```
